32 devices in a mesh: dp: 4 (over x, core), sp: 8 (over z, y).
Axes of the slice: x: 2, y: 2, z: 4, core: 2. Of those that a mesh axis runs over, the one named last changes fastest.
Arguments:
- tokens: bfloat16 [4, 2048, 768], P('dp', 'sp'), may hold values from -24 to 24
- cotangent: bfloat16 [4, 2048, 768], P('dp', 'sp'), may hold values from -6 to 6
- routes: int32 [4, 2048, 1], P('dp', 'sp'), may hold values from 0 to 3; in each aligned block of 256 rows (0 to 255, 256 to 511, ..., all dimensions but the last counted through in order) at most 128 rows name the same one
- buckets: int32 [4095], replicated, may hold values from 0 to 31, as said below
- gain_attn: bfloat16 [768], P('sp'), may hold values from 0.099609375 to 1.8984375
- w_qkv: bfloat16 [768, 2304], P('sp'), may hold values from -0.109375 to 0.109375
- w_out: bfloat16 [768, 768], P('sp'), may hold values from -2.5 to 2.5
- bias_table: bfloat16 [32, 12], replicated, may hold values from -4 to 4
- gain_ffn: bfloat16 [768], P('sp'), may hold values from 0.099609375 to 1.8984375
- router: bfloat16 [768, 4], P('sp'), may hold values from -0.15625 to 0.15625
- expert_in: bfloat16 [4, 768, 3072], P(None, 'sp'), may hold values from -0.21875 to 0.21875
- expert_out: bfloat16 [4, 3072, 768], P(None, 'sp'), may hold values from -0.75 to 0.75
Outputs:
- mixed: bfloat16 [4, 2048, 768], P('dp', 'sp')
- tokens_grad: float32 [4, 2048, 768], P('dp', 'sp')
- gain_attn_grad: float32 [768], P('sp')
- w_qkv_grad: float32 [768, 2304], P('sp')
- w_out_grad: float32 [768, 768], P('sp')
- bias_table_grad: float32 [32, 12], replicated
- gain_ffn_grad: float32 [768], P('sp')
- router_grad: float32 [768, 4], P('sp')
- expert_in_grad: float32 [4, 768, 3072], P(None, 'sp')
- expert_out_grad: float32 [4, 3072, 768], P(None, 'sp')
The draws below stay inside these ranges and needn't reach their ends.
Inputs may be any that keep to these rules, and one draw needn't show every extreme that they name: `routes`: each token names one expert; among the tokens of one device's piece of a sequence (aligned blocks of 2048 / 8 positions) no expert is named more than 128 times. `buckets`: entry r + 2047 is the bucket of the relative position r, key position minus query position.
All inputs are finite; a program needn't handle non-finite values.
Results may differ from the reference program's by a relative error of at most 0.02.
Values may be sent and summed in bfloat16 or wider, within the bound.
A program may use at most 256 MiB of HBM per device.

```python
import math
from functools import reduce
import jax
import jax.numpy as jnp
import numpy as np
from jax import lax

D = 768
H = 12
DH = 64
FF = 3072
BUCKETS = 32
EXPERTS = 4
LEN = 2048
BATCH = 4
CAP = 128
N_SP = 8


LIMITS = (12, 16, 23, 32, 46, 64, 91)


def draw_tokens(key, part):
    key = jax.random.fold_in(key, 11)
    key_main, key_rows, key_cols = jax.random.split(key, 3)
    full_shape = (BATCH, LEN, D)
    normal_part = jnp.clip(jax.random.normal(key_main, full_shape, jnp.float32), -4.0, 4.0)
    row_scales = jnp.exp(jax.random.uniform(key_rows, (BATCH, LEN, 1), jnp.float32, jnp.log(0.3), jnp.log(3.0)))
    column_scales = jnp.exp(jax.random.uniform(key_cols, (1, 1, D), jnp.float32, jnp.log(0.5), jnp.log(2.0)))
    return (normal_part * row_scales * column_scales).astype(jnp.bfloat16)


def draw_buckets(key, part):
    key = jax.random.fold_in(key, 5)
    offsets = jnp.arange(2 * LEN - 1, dtype=jnp.int32) - (LEN - 1)
    distance = jnp.abs(offsets)
    half_count = BUCKETS // 2
    exact_count = half_count // 2
    far_bucket = exact_count + reduce(lambda total, limit: total + (distance >= limit).astype(jnp.int32), LIMITS, jnp.zeros_like(distance))
    near_bucket = jnp.where(distance < exact_count, distance, far_bucket)
    base_bucket = near_bucket + jnp.where(offsets > 0, half_count, 0)
    ordering = jax.random.permutation(key, BUCKETS).astype(jnp.int32)
    return ordering[base_bucket].astype(jnp.int32)


def block_levels(own_key, shape, shards, low, high):
    factor_of, own = 1.0, jax.random.fold_in(own_key, 6)
    for position, shards_of in shards:
        draws = jnp.exp(jax.random.uniform(jax.random.fold_in(own, position), (shards_of,), jnp.float32, low / len(shards), high / len(shards)))
        factor_of = factor_of * jnp.repeat(draws, shape[position] // shards_of).reshape([-1 if axis == position else 1 for axis in range(len(shape))])
    return factor_of


def assign_block(key, own, number, rows, amount, top, bound, slope):
    order = jax.random.permutation(key, amount)
    crowded, common = shares(amount, rows * top, bound, slope, True), shares(amount, rows * top, bound, slope, False)
    places = jnp.arange(amount)

    def named(sizes, turn):
        used = int((sizes > 0).sum())
        fixed = max(1, used // 4)
        shifted = fixed + (places - fixed + turn * (used - fixed)) % max(1, amount - fixed)
        return jnp.zeros((amount,), jnp.int32).at[order[jnp.where(places < fixed, places, shifted)]].set(jnp.asarray(sizes, jnp.int32))

    sizes = jnp.where(number % 4 == 0, named(crowded, number // 4), named(common, number - number // 4 - 1))
    mixed = jax.random.permutation(jax.random.fold_in(own, 3), amount)
    donor, sink = mixed[0:amount // 2 * 2:2], mixed[1:amount // 2 * 2:2]
    room = jnp.minimum(sizes[donor] - 1, bound - sizes[sink]) // 2
    room = jnp.where((donor == order[0]) | (sink == order[0]) | (sizes[sink] == 0), 0, jnp.maximum(room, 0))
    shifted = jax.random.randint(jax.random.fold_in(own, 4), (amount // 2,), 0, 1 << 20) % (room + 1)
    sizes = sizes.at[donor].add(-shifted).at[sink].add(shifted)
    labels = jnp.searchsorted(jnp.cumsum(sizes), jnp.arange(rows * top), side="right").astype(jnp.int32)
    listing = labels.reshape(top, rows).T
    listing = listing[jax.random.permutation(jax.random.fold_in(own, 1), rows)]
    turn = jax.random.randint(jax.random.fold_in(own, 2), (rows, 1), 0, top)
    return jnp.take_along_axis(listing, (jnp.arange(top)[None, :] + turn) % top, axis=1)


def shares(number_of, total, reach, skew, full):
    weights = [(1 << 20) // math.isqrt(rank ** skew) + 1 for rank in range(1, number_of + 1)]
    largest = reach if full else min(reach, max(-(-total // number_of), total * weights[0] // sum(weights)))
    least = 1 if total - largest >= number_of - 1 else 0
    holding, surplus = [largest] + [least] * (number_of - 1), total - largest - least * (number_of - 1)
    while surplus > 0:
        free = [i for i in range(1, number_of) if holding[i] < largest] or [i for i in range(1, number_of) if holding[i] < reach]
        mass, remaining = sum([weights[i] for i in free]), surplus
        for i in free:
            more = min(reach - holding[i], max(1, remaining * weights[i] // mass), surplus)
            holding[i] = holding[i] + more
            surplus = surplus - more
    return np.array(holding)


def gaussian(stream_key, dims, spread, most, shards=(), kind=jnp.bfloat16):
    factor_of = block_levels(stream_key, dims, shards, -0.22, 0.18) if shards else 1.0
    array = jax.random.normal(stream_key, dims, jnp.float32) * spread * factor_of
    return jnp.minimum(jnp.maximum(array, -most), most).astype(kind)


def setup_inputs(seed: int = 0) -> dict:
    arg_keys = jax.random.split(jax.random.key(seed), 13)
    tokens = draw_tokens(jax.random.fold_in(arg_keys[12], 71), 0)
    cotangent = gaussian(arg_keys[1], (BATCH, LEN, D), 1.0, 6.0, ((0, 4), (1, 8)))
    routes_keys = jax.random.split(jax.random.fold_in(arg_keys[2], 1), BATCH * LEN // (LEN // N_SP))
    routes_turns = jax.random.permutation(jax.random.fold_in(arg_keys[2], 3), BATCH * LEN // (LEN // N_SP))
    routes = jax.vmap(lambda own, number: assign_block(jax.random.fold_in(arg_keys[2], 2), own, number, LEN // N_SP, EXPERTS, 1, CAP, 1))(routes_keys, routes_turns).reshape((BATCH, LEN, 1))
    buckets = draw_buckets(jax.random.fold_in(arg_keys[12], 71), 0)
    gain_attn = jnp.clip(1.0 + 0.18 * jax.random.normal(arg_keys[4], (D,), jnp.float32), 0.099609375, 1.8984375).astype(jnp.bfloat16)
    w_qkv = gaussian(arg_keys[5], (D, 3 * D), (4 * D) ** -0.5, 0.109375, ((0, 8),))
    w_out = gaussian(arg_keys[6], (D, D), (D // 128) ** -0.5, 2.5, ((0, 8),))
    bias_table = gaussian(arg_keys[7], (BUCKETS, H), 1.0, 4.0)
    gain_ffn = jnp.clip(1.0 + 0.18 * jax.random.normal(arg_keys[8], (D,), jnp.float32), 0.099609375, 1.8984375).astype(jnp.bfloat16)
    router = gaussian(arg_keys[9], (D, EXPERTS), (2 * D) ** -0.5, 0.15625, ((0, 8),))
    expert_in = gaussian(arg_keys[10], (EXPERTS, D, FF), D ** -0.5, 0.21875, ((1, 8),))
    expert_out = gaussian(arg_keys[11], (EXPERTS, FF, D), (FF // 48) ** -0.5, 0.75, ((1, 8),))
    return dict(tokens=tokens, cotangent=cotangent, routes=routes, buckets=buckets, gain_attn=gain_attn, w_qkv=w_qkv, w_out=w_out, bias_table=bias_table, gain_ffn=gain_ffn, router=router, expert_in=expert_in, expert_out=expert_out)


HIGHEST_PRECISION = lax.Precision.HIGHEST
epsilon = 1e-06

@jax.custom_vjp
def low(v):
    return lax.optimization_barrier(v.astype(jnp.bfloat16)).astype(jnp.float32)

@jax.custom_vjp
def low_back(v):
    return v

def low_keep(v):
    return (low(v), None)

def low_pass(kept, grad):
    return (grad,)

def back_keep(v):
    return (v, None)

def back_low(kept, grad):
    return (low(grad),)
low.defvjp(low_keep, low_pass)
low_back.defvjp(back_keep, back_low)

def rms_scale(values):
    return lax.rsqrt(lax.optimization_barrier(jnp.mean(values * values, axis=-1, keepdims=True)) + epsilon)

def one_sequence(inputs, route, weights_all, bias):
    gain_one, w_qkv, w_out, gain_two, router, expert_in, expert_out = weights_all
    heads = bias.shape[0]
    width = inputs.shape[1]
    piece = LEN // N_SP
    normed_one = low(inputs * rms_scale(inputs) * gain_one)
    projected = low_back(low(jnp.dot(normed_one, w_qkv, precision=HIGHEST_PRECISION)))
    queries = projected[:, :width].reshape(LEN, heads, DH)
    keys = projected[:, width:2 * width].reshape(LEN, heads, DH)
    values = projected[:, 2 * width:].reshape(LEN, heads, DH)
    scores = low_back(jnp.einsum('ihd,jhd->hij', queries, keys, precision=HIGHEST_PRECISION) + bias)
    probs = jax.nn.softmax(scores, axis=-1)
    attended = jnp.einsum('hij,jhd->ihd', low(probs), values, precision=HIGHEST_PRECISION).reshape(LEN, width)
    attended = low_back(low(attended))
    middle = inputs + low_back(jnp.dot(attended, w_out, precision=HIGHEST_PRECISION))
    normed_two = low(middle * rms_scale(middle) * gain_two)
    gates_all = jax.nn.softmax(jnp.dot(normed_two, router, precision=HIGHEST_PRECISION), axis=-1)
    chosen_int = (route == jnp.arange(EXPERTS, dtype=jnp.int32)[None, :]).astype(jnp.int32)
    gate = lax.optimization_barrier(jnp.sum(gates_all * chosen_int.astype(gates_all.dtype), axis=-1, keepdims=True))
    pieces = chosen_int.reshape(N_SP, piece, EXPERTS)
    place = lax.optimization_barrier(jnp.sum((jnp.cumsum(pieces, axis=1) - 1) * pieces, axis=-1))
    slots = (place[:, :, None] == jnp.arange(CAP, dtype=jnp.int32)[None, None, :]).astype(inputs.dtype)
    dispatch = pieces.astype(inputs.dtype)[:, :, :, None] * slots[:, :, None, :]
    buffers = jnp.einsum('ntec,ntd->necd', dispatch, normed_two.reshape(N_SP, piece, width), precision=HIGHEST_PRECISION)
    hidden_in = low_back(jnp.einsum('necd,edf->necf', buffers, expert_in, precision=HIGHEST_PRECISION))
    activated = low(jax.nn.gelu(hidden_in))
    expert_outs = low_back(jnp.einsum('necf,efd->necd', activated, expert_out, precision=HIGHEST_PRECISION))
    returned = jnp.einsum('ntec,necd->ntd', dispatch, expert_outs, precision=HIGHEST_PRECISION).reshape(LEN, width)
    return middle + gate * returned

def layer(inputs, gain_one, w_qkv, w_out, bias_table, gain_two, router, expert_in, expert_out, routes, buckets):
    positions = jnp.arange(LEN, dtype=jnp.int32)
    offsets = positions[None, :] - positions[:, None] + (LEN - 1)
    per_offset = jnp.take(bias_table, buckets, axis=0)
    bias = jnp.transpose(jnp.take(per_offset, offsets, axis=0), (2, 0, 1))
    weights_all = (gain_one, w_qkv, w_out, gain_two, router, expert_in, expert_out)
    per_sequence = jax.checkpoint(lambda operands: one_sequence(operands[0], operands[1], weights_all, bias))
    return lax.map(per_sequence, (inputs, routes))

def reference(tokens, cotangent, routes, buckets, gain_attn, w_qkv, w_out, bias_table, gain_ffn, router, expert_in, expert_out):

    def forward(inputs, gain_one, w_first, w_second, table_f, gain_two, router_f, first_f, second_f):
        return layer(inputs, gain_one, w_first, w_second, table_f, gain_two, router_f, first_f, second_f, routes, buckets)
    mixed, pull_back = jax.vjp(forward, tokens.astype(jnp.float32), gain_attn.astype(jnp.float32), w_qkv.astype(jnp.float32), w_out.astype(jnp.float32), bias_table.astype(jnp.float32), gain_ffn.astype(jnp.float32), router.astype(jnp.float32), expert_in.astype(jnp.float32), expert_out.astype(jnp.float32))
    grads = pull_back(cotangent.astype(jnp.float32))
    return (mixed.astype(jnp.bfloat16), grads[0], grads[1], grads[2], grads[3], grads[4], grads[5], grads[6], grads[7], grads[8])
```

```python
import jax
import jax.numpy as jnp
from jax import lax
from jax.sharding import PartitionSpec as P

HIGHEST_PRECISION = lax.Precision.HIGHEST
epsilon = 1e-06


def rms_scale(values):
    return lax.rsqrt(jnp.mean(values * values, axis=-1, keepdims=True) + epsilon)


def norm_back(values, scale, gain, grad_out):
    weighted = gain * grad_out
    grad_in = scale * weighted - values * scale**3 * jnp.mean(
        weighted * values, axis=-1, keepdims=True
    )
    grad_gain = jnp.sum(grad_out * values * scale, axis=(0, 1))
    return (grad_in, grad_gain)


def toeplitz(window, rows, columns):
    inner = 16
    reach = columns + rows - inner
    near = jnp.stack([window[inner - 1 - b : inner - 1 - b + reach] for b in range(inner)])
    far = [
        near[:, rows - inner - inner * a : rows - inner - inner * a + columns]
        for a in range(rows // inner)
    ]
    return jnp.concatenate(far, axis=0)


def bucket_onehot(buckets, count, query_start, query_count, key_count):
    window = lax.dynamic_slice(
        buckets, (key_count - query_start - query_count,), (key_count + query_count - 1,)
    )
    pair_buckets = toeplitz(window, query_count, key_count)
    return (pair_buckets[:, :, None] == jnp.arange(count, dtype=jnp.int32)[None, None, :]).astype(
        jnp.bfloat16
    )


def columns_of(values):
    return jnp.pad(values, ((0, 0), (0, -values.shape[1] % 128)))


def split_heads(values, heads):
    return values.reshape(values.shape[0], values.shape[1], heads, values.shape[2] // heads)


def body(
    tokens,
    cotangent,
    routes,
    buckets,
    gain_attn,
    w_qkv,
    w_out,
    bias_table,
    gain_ffn,
    router,
    expert_in,
    expert_out,
):
    heads = bias_table.shape[1]
    bucket_count = bias_table.shape[0]
    seq_count, piece, width = tokens.shape
    experts = router.shape[1]
    sequences = lax.axis_size("dp")
    team = min(sequences, experts)
    share = experts // team
    first = lax.rem(lax.axis_index("dp"), team) * share
    teams = None
    if team < sequences:
        teams = [list(range(t, t + team)) for t in range(0, sequences, team)]
    packed = lax.all_gather(
        jnp.concatenate(
            (w_qkv, w_out, columns_of(jnp.concatenate((gain_attn[:, None], gain_ffn[:, None], router), 1))),
            axis=1,
        ),
        "sp",
        axis=0,
        tiled=True,
    )
    attn_set = (packed[:, 4 * width], packed[:, : 3 * width], packed[:, 3 * width : 4 * width])
    ffn_set = (
        packed[:, 4 * width + 1],
        packed[:, 4 * width + 2 : 4 * width + 2 + experts],
        lax.all_gather(
            lax.dynamic_slice_in_dim(expert_in, first, share, 0), "sp", axis=1, tiled=True
        ),
        lax.all_gather(
            lax.dynamic_slice_in_dim(expert_out, first, share, 0), "sp", axis=1, tiled=True
        ),
    )
    inputs = tokens.astype(jnp.float32)
    scale_one = rms_scale(inputs)
    normed_one = (inputs * scale_one * attn_set[0].astype(jnp.float32)).astype(jnp.bfloat16)
    projected = jnp.einsum(
        "spd,de->spe", normed_one, attn_set[1], preferred_element_type=jnp.float32
    ).astype(jnp.bfloat16)
    queries = projected[:, :, :width]
    keys_values = lax.all_gather(projected[:, :, width:], "sp", axis=1, tiled=True)
    keys_all, values_all = keys_values[:, :, :width], keys_values[:, :, width:]
    length = keys_all.shape[1]
    start = lax.axis_index("sp") * piece
    near_onehot = bucket_onehot(buckets, bucket_count, start, piece, length)
    bias_rows = jnp.einsum(
        "ijc,ch->hij", near_onehot, bias_table, preferred_element_type=jnp.float32
    )
    query_heads = split_heads(queries, heads)
    scores = (
        jnp.einsum(
            "sihd,sjhd->shij",
            query_heads,
            split_heads(keys_all, heads),
            preferred_element_type=jnp.float32,
        )
        + bias_rows[None]
    )
    top_score = jnp.max(scores, axis=-1, keepdims=True)
    log_total = top_score + jnp.log(jnp.sum(jnp.exp(scores - top_score), axis=-1, keepdims=True))
    probs_low = jnp.exp(scores - log_total).astype(jnp.bfloat16)
    attended = jnp.einsum(
        "shij,sjhd->sihd",
        probs_low,
        split_heads(values_all, heads),
        preferred_element_type=jnp.float32,
    )
    attended = attended.reshape(seq_count, piece, width).astype(jnp.bfloat16)
    middle = inputs + jnp.einsum(
        "spd,de->spe", attended, attn_set[2], preferred_element_type=jnp.float32
    )
    gain_two = ffn_set[0].astype(jnp.float32)
    scale_two = rms_scale(middle)
    normed_two = (middle * scale_two * gain_two).astype(jnp.bfloat16)
    logits = jnp.einsum("spd,de->spe", normed_two, ffn_set[1], preferred_element_type=jnp.float32)
    gates_all = jax.nn.softmax(logits, axis=-1)
    chosen_int = (routes == jnp.arange(experts, dtype=jnp.int32)[None, None, :]).astype(jnp.int32)
    chosen = chosen_int.astype(jnp.float32)
    gate = jnp.sum(gates_all * chosen, axis=-1, keepdims=True)
    capacity = 2 * piece // experts
    place = jnp.sum((jnp.cumsum(chosen_int, axis=1) - 1) * chosen_int, axis=-1)
    slots = (place[:, :, None] == jnp.arange(capacity, dtype=jnp.int32)[None, None, :]).astype(
        jnp.float32
    )
    dispatch_low = (chosen[:, :, :, None] * slots[:, :, None, :]).astype(jnp.bfloat16)
    grad_out = cotangent.astype(jnp.float32)
    grad_returned = (gate * grad_out).astype(jnp.bfloat16)
    sent = jnp.einsum(
        "stec,std->escd",
        dispatch_low,
        jnp.concatenate((normed_two, grad_returned), axis=-1),
        preferred_element_type=jnp.float32,
    ).astype(jnp.bfloat16)
    held = lax.all_to_all(
        sent.reshape(experts, seq_count * capacity, 2 * width),
        "dp",
        0,
        1,
        axis_index_groups=teams,
        tiled=True,
    )
    buffers, grad_outs = held[:, :, :width], held[:, :, width:]
    hidden_in = jnp.einsum("ecd,edf->ecf", buffers, ffn_set[2], preferred_element_type=jnp.float32)
    activated = jax.nn.gelu(hidden_in).astype(jnp.bfloat16)
    expert_outs = jnp.einsum(
        "ecf,efd->ecd", activated, ffn_set[3], preferred_element_type=jnp.float32
    )
    grad_act = jnp.einsum(
        "ecd,efd->ecf", grad_outs, ffn_set[3], preferred_element_type=jnp.float32
    )
    grad_hidden = jax.vjp(jax.nn.gelu, hidden_in)[1](grad_act)[0].astype(jnp.bfloat16)
    grad_buffers = jnp.einsum(
        "ecf,edf->ecd", grad_hidden, ffn_set[2], preferred_element_type=jnp.float32
    )
    back = lax.all_to_all(
        jnp.concatenate((expert_outs, grad_buffers), axis=-1).astype(jnp.bfloat16),
        "dp",
        1,
        0,
        axis_index_groups=teams,
        tiled=True,
    )
    grad_w_down = jnp.einsum(
        "ecf,ecd->efd", activated, grad_outs, preferred_element_type=jnp.float32
    )
    grad_w_up = jnp.einsum(
        "ecd,ecf->edf", buffers, grad_hidden, preferred_element_type=jnp.float32
    )
    taken = jnp.einsum(
        "stec,escd->std",
        dispatch_low,
        back.reshape(experts, seq_count, capacity, 2 * width),
        preferred_element_type=jnp.float32,
    )
    returned, grad_normed_two = taken[:, :, :width], taken[:, :, width:]
    mixed = (middle + gate * returned).astype(jnp.bfloat16)
    grad_gate = jnp.sum(grad_out * returned, axis=-1, keepdims=True)
    grad_logits = grad_gate * gate * (chosen - gates_all)
    grad_router = jnp.einsum(
        "spd,spe->de", normed_two.astype(jnp.float32), grad_logits, precision=HIGHEST_PRECISION
    )
    grad_normed_two = grad_normed_two + jnp.einsum(
        "spe,de->spd", grad_logits, ffn_set[1].astype(jnp.float32), precision=HIGHEST_PRECISION
    )
    grad_middle, grad_gain_two = norm_back(
        middle, scale_two, ffn_set[0].astype(jnp.float32), grad_normed_two
    )
    grad_middle = grad_out + grad_middle
    grad_branch = grad_middle.astype(jnp.bfloat16)
    grad_w_out = jnp.einsum(
        "spd,spe->de", attended, grad_branch, preferred_element_type=jnp.float32
    )
    up_share = lax.psum_scatter(
        grad_w_up.astype(jnp.bfloat16), "sp", scatter_dimension=1, tiled=True
    )
    down_share = lax.psum_scatter(
        grad_w_down.astype(jnp.bfloat16), "sp", scatter_dimension=1, tiled=True
    )
    early = lax.psum_scatter(
        jnp.concatenate(
            (
                grad_w_out.astype(jnp.bfloat16),
                columns_of(
                    jnp.concatenate((grad_gain_two[:, None], grad_router), 1).astype(jnp.bfloat16)
                ),
            ),
            axis=1,
        ),
        "sp",
        scatter_dimension=0,
        tiled=True,
    )
    grad_attended = jnp.einsum(
        "spe,de->spd", grad_branch, attn_set[2], preferred_element_type=jnp.float32
    ).astype(jnp.bfloat16)
    grad_heads = split_heads(grad_attended, heads)
    key_heads = split_heads(keys_all, heads)
    value_heads = split_heads(values_all, heads)
    scores_back = (
        jnp.einsum("sihd,sjhd->shij", query_heads, key_heads, preferred_element_type=jnp.float32)
        + bias_rows[None]
    )
    probs_back = jnp.exp(scores_back - log_total)
    grad_probs = jnp.einsum(
        "sihd,sjhd->shij", grad_heads, value_heads, preferred_element_type=jnp.float32
    )
    row_dot = jnp.sum(probs_back * grad_probs, axis=-1, keepdims=True)
    grad_scores = (probs_back * (grad_probs - row_dot)).astype(jnp.bfloat16)
    grad_queries = jnp.einsum(
        "shij,sjhd->sihd", grad_scores, key_heads, preferred_element_type=jnp.float32
    )
    grad_queries = grad_queries.reshape(seq_count, piece, width).astype(jnp.bfloat16)
    grad_table = jnp.einsum(
        "shij,ijc->ch", grad_scores, near_onehot, preferred_element_type=jnp.float32
    )
    grad_keys_part = jnp.einsum(
        "shij,sihd->sjhd", grad_scores, query_heads, preferred_element_type=jnp.float32
    )
    grad_values_part = jnp.einsum(
        "shij,sihd->sjhd",
        probs_back.astype(jnp.bfloat16),
        grad_heads,
        preferred_element_type=jnp.float32,
    )
    grad_keys_values = lax.psum_scatter(
        jnp.concatenate(
            (
                grad_keys_part.reshape(seq_count, length, width),
                grad_values_part.reshape(seq_count, length, width),
            ),
            axis=-1,
        ).astype(jnp.bfloat16),
        "sp",
        scatter_dimension=1,
        tiled=True,
    )
    grad_projected = jnp.concatenate((grad_queries, grad_keys_values), axis=-1)
    grad_w_qkv = jnp.einsum(
        "spd,spe->de", normed_one, grad_projected, preferred_element_type=jnp.float32
    )
    grad_normed_one = jnp.einsum(
        "spe,de->spd", grad_projected, attn_set[1], preferred_element_type=jnp.float32
    )
    grad_inputs, grad_gain_one = norm_back(
        inputs, scale_one, attn_set[0].astype(jnp.float32), grad_normed_one
    )
    grad_inputs = grad_middle + grad_inputs
    late = lax.psum_scatter(
        jnp.concatenate(
            (grad_w_qkv.astype(jnp.bfloat16), columns_of(grad_gain_one[:, None].astype(jnp.bfloat16))),
            axis=1,
        ),
        "sp",
        scatter_dimension=0,
        tiled=True,
    )
    grad_up, grad_down = (
        jnp.sum(
            lax.all_gather(each, "dp", axis=0, tiled=True)
            .reshape(sequences // team, experts, *each.shape[1:])
            .astype(jnp.float32),
            axis=0,
        )
        for each in (up_share, down_share)
    )
    early = lax.psum(early, "dp").astype(jnp.float32)
    late = lax.psum(late, "dp").astype(jnp.float32)
    table_total = lax.psum(grad_table, ("dp", "sp"))
    return (
        mixed,
        grad_inputs,
        late[:, 3 * width],
        late[:, : 3 * width],
        early[:, :width],
        table_total,
        early[:, width],
        early[:, width + 1 : width + 1 + experts],
        grad_up,
        grad_down,
    )


def solution(mesh):
    return jax.shard_map(
        body,
        mesh=mesh,
        in_specs=(
            P("dp", "sp", None),
            P("dp", "sp", None),
            P("dp", "sp", None),
            P(),
            P("sp"),
            P("sp", None),
            P("sp", None),
            P(),
            P("sp"),
            P("sp", None),
            P(None, "sp", None),
            P(None, "sp", None),
        ),
        out_specs=(
            P("dp", "sp", None),
            P("dp", "sp", None),
            P("sp"),
            P("sp", None),
            P("sp", None),
            P(),
            P("sp"),
            P("sp", None),
            P(None, "sp", None),
            P(None, "sp", None),
        ),
        check_vma=False,
    )
```
